32 devices in a mesh: groups: 2 (over y), tenant: 4 (over x, core), tensor: 4 (over z).
Axes of the slice: x: 2, y: 2, z: 4, core: 2. Of those that a mesh axis runs over, the one named last changes fastest.
Arguments:
- feats: bfloat16 [1024, 8192], P(('groups', 'tenant'), 'tensor'), parts along dimension 0, may hold values from -6 to 6
- gate_preactivation: bfloat16 [1024, 14784], P(('groups', 'tenant'), 'tensor'), parts along dimension 0, may hold values from -8 to 8
- row_loss_curvature: bfloat16 [1024], P(('groups', 'tenant')), parts along dimension 0, may hold values from 0.25 to 4
- row_adapter_index: int32 [1024], P(('groups', 'tenant')), parts along dimension 0, may hold values from 0 to 15, as said below
- row_adapter_position: int32 [1024], P(('groups', 'tenant')), parts along dimension 0, may hold values from 0 to 31, as said below
- down_projection_weight: bfloat16 [14784, 8192], P('tensor'), may hold values from -0.0625 to 0.0625
- adapter_input_factors: bfloat16 [32, 8192, 32], P(('groups', 'tenant'), 'tensor'), parts along dimension 0, may hold values from -6 to 6
- adapter_output_factors: bfloat16 [32, 32, 14784], P(('groups', 'tenant'), None, 'tensor'), parts along dimension 0, may hold values from -6 to 6
- iterate_input_factors: float32 [32, 8192, 32], P(('groups', 'tenant'), 'tensor'), parts along dimension 0, may hold values from -6 to 6
- iterate_output_factors: float32 [32, 32, 14784], P(('groups', 'tenant'), None, 'tensor'), parts along dimension 0, may hold values from -6 to 6
- input_factor_gradient: float32 [32, 8192, 32], P(('groups', 'tenant'), 'tensor'), parts along dimension 0, may hold values from -6 to 6
- output_factor_gradient: float32 [32, 32, 14784], P(('groups', 'tenant'), None, 'tensor'), parts along dimension 0, may hold values from -6 to 6
Outputs:
- new_a: float32 [32, 8192, 32], P(('groups', 'tenant'), 'tensor'), parts along dimension 0
- new_b: float32 [32, 32, 14784], P(('groups', 'tenant'), None, 'tensor'), parts along dimension 0
- row_cot: bfloat16 [1024, 8192], P(('groups', 'tenant'), 'tensor'), parts along dimension 0
The draws below stay inside these ranges and needn't reach their ends.
There are 2 independent parts, one for each index of `groups`. The reference program is written for one: setup_inputs(seed, part) draws one part's arguments, and reference() takes and returns one part's arrays. A program takes and returns all parts, laid end to end along the dimension named above; an argument that names none is the same for every part. Nothing has to cross between parts.
Inputs may be any that keep to these rules, and one draw needn't show every extreme that they name: `row_adapter_index`: every device of the tenant axis holds exactly 8 rows of each adapter. `row_adapter_position`: the rows of one adapter carry each slot exactly once.
All inputs are finite; a program needn't handle non-finite values.
Results may differ from the reference program's by a relative error of at most 0.0053.
Values may be sent and summed in bfloat16 or wider, within the bound.
A program may use at most 192 MiB of HBM per device.

```python
import math
import jax
import jax.numpy as jnp
from jax import lax

MODEL_WIDTH = 8192
HIDDEN_UNITS = 14784
ADAPTER_RANK = 32
SEND = 8
ROWS_TEN = 32
ROWS = 128
ADAPTER_COUNT = 16
ALLROWS = 512


def layout(key):
    sources = ALLROWS // ROWS
    first, second = jax.random.split(key)
    base_ids = jnp.repeat(jnp.arange(ADAPTER_COUNT, dtype=jnp.int32), SEND)
    shuffles = jax.vmap(lambda k: jax.random.permutation(k, ADAPTER_COUNT * SEND))(jax.random.split(first, sources))
    slot_orders = jax.vmap(lambda k: jax.random.permutation(k, ROWS_TEN))(jax.random.split(second, ADAPTER_COUNT))
    owners = base_ids[shuffles]
    within = shuffles % SEND
    source_idx = jnp.arange(sources, dtype=jnp.int32)[:, None]
    slots = slot_orders[owners, source_idx * SEND + within]
    return (owners.reshape(-1).astype(jnp.int32), slots.reshape(-1).astype(jnp.int32))


def draw_row_adapter_index(key, part):
    return layout(key)[0]


def draw_row_adapter_position(key, part):
    return layout(key)[1]


def strengthened(values, rng, source, target, blocks, factor):
    def block_of(position):
        return (jnp.arange(values.shape[position]) // (values.shape[position] // blocks)).reshape((-1,) + (1,) * (values.ndim - 1 - position))

    one_side = jax.random.permutation(rng, blocks)[block_of(target)]
    second = (block_of(target) + blocks // 2) % blocks
    return jnp.where((block_of(source) == one_side) | (block_of(source) == second), factor * values, values)


def block_levels(stream_key, dims, cuts, low, largest):
    gain = 1.0
    for axis_at, blocks in cuts:
        draws = jax.random.uniform(jax.random.fold_in(jax.random.fold_in(stream_key, 6), axis_at), (blocks,), jnp.float32, low / len(cuts), largest / len(cuts))
        gain = gain * jnp.repeat(jnp.exp(draws), dims[axis_at] // blocks).reshape((-1,) + (1,) * (len(dims) - 1 - axis_at))
    return gain


def centred(stream_key, extent, scale, limit, cuts=(), kind=jnp.bfloat16):
    loudness = block_levels(stream_key, extent, cuts, -0.22, 0.18) if cuts else 1.0
    drawn = jax.random.normal(stream_key, extent, jnp.float32) * scale * loudness
    return jnp.minimum(jnp.maximum(drawn, -limit), limit).astype(kind)


def bell_draw_with(rng, extent, spread, reach, shards, heavy, kind=jnp.bfloat16):
    drawn = spread * jax.random.normal(rng, extent, jnp.float32)
    if shards:
        drawn = drawn * block_levels(rng, extent, shards, -0.22, 0.18)
    return jnp.clip(strengthened(drawn, jax.random.fold_in(rng, 3), *heavy), -reach, reach).astype(kind)


def setup_inputs(seed: int = 0, part: int = 0) -> dict:
    keys = jax.random.split(jax.random.key(seed), 13)
    own_keys = jax.random.split(jax.random.fold_in(keys[12], part), 13)
    return {
        "feats": centred(own_keys[0], (ALLROWS, MODEL_WIDTH), 1.0, 6.0, ((0, 4), (1, 4))),
        "gate_preactivation": centred(own_keys[1], (ALLROWS, HIDDEN_UNITS), 1.5, 8.0, ((0, 4), (1, 4))),
        "row_loss_curvature": jnp.clip(jnp.exp(math.log(4.0) - 2.7725887 * jax.random.uniform(own_keys[2], (ALLROWS,), jnp.float32) ** block_levels(own_keys[2], (ALLROWS,), ((0, 4),), -0.2, 0.2)), 0.25, 4.0).astype(jnp.bfloat16),
        "row_adapter_index": draw_row_adapter_index(jax.random.fold_in(jax.random.fold_in(keys[12], part), 71), part),
        "row_adapter_position": draw_row_adapter_position(jax.random.fold_in(jax.random.fold_in(keys[12], part), 71), part),
        "down_projection_weight": bell_draw_with(keys[5], (HIDDEN_UNITS, MODEL_WIDTH), HIDDEN_UNITS ** -0.5, 0.0625, ((0, 4),), (0, 1, 4, 2.0)),
        "adapter_input_factors": centred(own_keys[6], (ADAPTER_COUNT, MODEL_WIDTH, ADAPTER_RANK), 1.0, 6.0, ((0, 4), (1, 4))),
        "adapter_output_factors": centred(own_keys[7], (ADAPTER_COUNT, ADAPTER_RANK, HIDDEN_UNITS), 1.0, 6.0, ((0, 4), (2, 4))),
        "iterate_input_factors": centred(own_keys[8], (ADAPTER_COUNT, MODEL_WIDTH, ADAPTER_RANK), 1.0, 6.0, ((0, 4), (1, 4)), jnp.float32),
        "iterate_output_factors": centred(own_keys[9], (ADAPTER_COUNT, ADAPTER_RANK, HIDDEN_UNITS), 1.0, 6.0, ((0, 4), (2, 4)), jnp.float32),
        "input_factor_gradient": centred(own_keys[10], (ADAPTER_COUNT, MODEL_WIDTH, ADAPTER_RANK), 1.0, 6.0, ((0, 4), (1, 4)), jnp.float32),
        "output_factor_gradient": centred(own_keys[11], (ADAPTER_COUNT, ADAPTER_RANK, HIDDEN_UNITS), 1.0, 6.0, ((0, 4), (2, 4)), jnp.float32),
    }


damping = 0.05
lissa_scale = 2.0

def reference(feats, gate_preactivation, row_loss_curvature, row_adapter_index, row_adapter_position, down_projection_weight, adapter_input_factors, adapter_output_factors, iterate_input_factors, iterate_output_factors, input_factor_gradient, output_factor_gradient):
    highest_precision = lax.Precision.HIGHEST
    grouped_place = (row_adapter_index * ROWS_TEN + row_adapter_position).astype(jnp.int32)
    grouped_order = jnp.zeros((ALLROWS,), jnp.int32).at[grouped_place].set(jnp.arange(ALLROWS, dtype=jnp.int32))
    grouped_input_rows = feats[grouped_order].reshape(ADAPTER_COUNT, ROWS_TEN, MODEL_WIDTH).astype(jnp.float32)
    gate_vals = gate_preactivation[grouped_order].reshape(ADAPTER_COUNT, ROWS_TEN, HIDDEN_UNITS).astype(jnp.float32)
    weights = row_loss_curvature[grouped_order].astype(jnp.float32)
    project_rows = jnp.einsum('ake,aex->akx', grouped_input_rows, adapter_input_factors.astype(jnp.float32), precision=highest_precision) / math.sqrt(MODEL_WIDTH)
    lowrank_tangent = jnp.einsum('ake,aex->akx', grouped_input_rows, iterate_input_factors, precision=highest_precision) / math.sqrt(MODEL_WIDTH)
    up_tangent = (jnp.einsum('wqh,whx->wqx', lowrank_tangent, adapter_output_factors.astype(jnp.float32), precision=highest_precision) + jnp.einsum('wqh,whx->wqx', project_rows, iterate_output_factors, precision=highest_precision)) / math.sqrt(ADAPTER_RANK)
    gate_act = jax.nn.silu(gate_vals)
    hidden_tan = (gate_act * up_tangent).astype(jnp.bfloat16).reshape(ALLROWS, HIDDEN_UNITS)
    out_tan = jnp.dot(hidden_tan, down_projection_weight, preferred_element_type=jnp.float32)
    cotangent = (weights[:, None] * out_tan).astype(jnp.bfloat16)
    hidden_bar = jnp.dot(cotangent, down_projection_weight.T, preferred_element_type=jnp.float32).reshape(ADAPTER_COUNT, ROWS_TEN, HIDDEN_UNITS)
    up_cotangent = (gate_act * hidden_bar).astype(jnp.bfloat16).astype(jnp.float32)
    lowrank_backward = jnp.einsum('acv,apv->acp', up_cotangent, adapter_output_factors.astype(jnp.float32), precision=highest_precision) / math.sqrt(ADAPTER_RANK)
    curve_a = jnp.einsum('tsd,tsr->tdr', grouped_input_rows, lowrank_backward, precision=highest_precision) / math.sqrt(MODEL_WIDTH)
    curvature_output_factor = jnp.einsum('bji,bjw->biw', project_rows, up_cotangent, precision=highest_precision) / math.sqrt(ADAPTER_RANK)
    new_a = input_factor_gradient + (1.0 - damping) * iterate_input_factors - curve_a / lissa_scale
    new_b = output_factor_gradient + (1.0 - damping) * iterate_output_factors - curvature_output_factor / lissa_scale
    return (new_a, new_b, cotangent)
```

```python
import functools
import math

import jax
import jax.numpy as jnp
from jax import lax
from jax.experimental import pallas as pl
from jax.experimental.pallas import tpu as pltpu
from jax.sharding import PartitionSpec as P

MODEL_WIDTH = 8192
ADAPTER_RANK = 32


damping = 0.05
lissa_scale = 2.0


LINE = 4
COLS = 256
MESH = pl.DeviceIdType.MESH


def line_kernel(
    nb, resident, streams,
    h_ref, w_ref, gate_ref, weight_ref, cot_ref, e_ref,
    wbuf, y, from_left, from_right, outgoing, cot, acc,
    wsem, left_sem, right_sem, sum_send, cot_sem, cot_send_right, cot_send_left,
):
    n = LINE
    me = lax.axis_index("tensor")
    share = nb * COLS
    hidden = h_ref.shape[1]
    streamed = nb - resident

    def fetch(slot, b, q):
        cols = pl.ds(pl.multiple_of(q * share + b * COLS, COLS), COLS)
        return pltpu.make_async_copy(
            weight_ref.at[:, cols], wbuf.at[slot, :, pl.ds(q * COLS, COLS)], wsem.at[slot, q]
        )

    def sum_copy(b, q, to_right):
        return pltpu.make_async_remote_copy(
            src_ref=outgoing.at[b, q],
            dst_ref=(from_left if to_right else from_right).at[b, q],
            send_sem=sum_send.at[b, q],
            recv_sem=(left_sem if to_right else right_sem).at[b, q],
            device_id={"tensor": me + 1 if to_right else me - 1},
            device_id_type=MESH,
        )

    def cot_copy(b, o, to_right):
        block = cot.at[b, :, pl.ds(o * COLS, COLS)]
        return pltpu.make_async_remote_copy(
            src_ref=block,
            dst_ref=block,
            send_sem=(cot_send_right if to_right else cot_send_left).at[b, o],
            recv_sem=cot_sem.at[b, o],
            device_id={"tensor": me + 1 if to_right else me - 1},
            device_id_type=MESH,
        )

    for b in range(resident):
        for q in range(n):
            fetch(b, b, q).start()
    for u in range(streams):
        for q in range(n):
            fetch(resident + u, resident + u, q).start()

    barrier = pltpu.get_barrier_semaphore()
    for neighbour in (lax.rem(me + 1, n), lax.rem(me + n - 1, n)):
        pl.semaphore_signal(barrier, inc=1, device_id={"tensor": neighbour}, device_id_type=MESH)
    pl.semaphore_wait(barrier, 2)

    acc[...] = jnp.zeros_like(acc)

    def advance_sums(i):
        for q in range(n):
            hops = jnp.where(
                me < q, me, jnp.where(me > q, n - 1 - me, jnp.maximum(me, n - 1 - me))
            )
            b = i - 1 - hops

            @pl.when((b >= 0) & (b < nb))
            def _():
                @pl.when((me <= q) & (me > 0))
                def _():
                    sum_copy(b, q, True).wait_recv()
                    y[b, q] += from_left[b, q].astype(jnp.float32)

                @pl.when((me >= q) & (me < n - 1))
                def _():
                    sum_copy(b, q, False).wait_recv()
                    y[b, q] += from_right[b, q].astype(jnp.float32)

                @pl.when(me < q)
                def _():
                    outgoing[b, q] = y[b, q].astype(jnp.bfloat16)
                    sum_copy(b, q, True).start()

                @pl.when(me > q)
                def _():
                    outgoing[b, q] = y[b, q].astype(jnp.bfloat16)
                    sum_copy(b, q, False).start()

                @pl.when(me == q)
                def _():
                    block = (w_ref[...] * y[b, q]).astype(jnp.bfloat16)
                    cot[b, :, q * COLS : (q + 1) * COLS] = block
                    cot_ref[:, pl.ds(pl.multiple_of(b * COLS, COLS), COLS)] = block

                    @pl.when(me < n - 1)
                    def _():
                        cot_copy(b, q, True).start()

                    @pl.when(me > 0)
                    def _():
                        cot_copy(b, q, False).start()

    def advance_cots(i):
        for o in range(n):
            b = i - 1 - max(o, n - 1 - o) - jnp.abs(me - o)

            @pl.when((b >= 0) & (b < nb) & (me != o))
            def _():
                cot_copy(b, o, True).wait_recv()

                @pl.when((me > o) & (me < n - 1))
                def _():
                    cot_copy(b, o, True).start()

                @pl.when((me < o) & (me > 0))
                def _():
                    cot_copy(b, o, False).start()

    def refill(u):
        later = u + streams

        @pl.when((u >= 0) & (later < 2 * streamed))
        def _():
            for q in range(n):
                fetch(resident + later % streams, resident + later % streamed, q).start()

    last_lag = 2 * n - 1

    def step(i, carry):
        advance_sums(i)
        advance_cots(i)

        @pl.when(i < nb)
        def _():
            u = i - resident
            slot = jnp.where(u < 0, i, resident + jnp.maximum(u, 0) % streams)
            for q in range(n):
                fetch(slot, i, q).wait()
                y[i, q] = jnp.dot(
                    h_ref[...],
                    wbuf[slot, :, q * COLS : (q + 1) * COLS],
                    preferred_element_type=jnp.float32,
                )
            refill(u)

        @pl.when(i >= last_lag)
        def _():
            b = i - last_lag
            u = b - resident
            slot = jnp.where(u < 0, b, resident + (jnp.maximum(u, 0) + streamed) % streams)

            @pl.when(u >= 0)
            def _():
                for q in range(n):
                    fetch(slot, b, q).wait()

            for start in range(0, hidden, 512):
                size = min(512, hidden - start)
                acc[:, start : start + size] += lax.dot_general(
                    cot[b],
                    wbuf[slot, start : start + size, :],
                    (((1,), (1,)), ((), ())),
                    preferred_element_type=jnp.float32,
                )

            @pl.when(u >= 0)
            def _():
                refill(u + streamed)

        return carry

    lax.fori_loop(0, nb + last_lag, step, 0)

    for start in range(0, hidden, 512):
        size = min(512, hidden - start)
        gate = gate_ref[:, start : start + size].astype(jnp.float32)
        e_ref[:, start : start + size] = (
            gate / (1.0 + jnp.exp(-gate)) * acc[:, start : start + size]
        ).astype(jnp.bfloat16)

    def drain(b, carry):
        for q in range(n):
            @pl.when(me != q)
            def _():
                sum_copy(b, q, True).wait_send()

            @pl.when((q <= me) & (me < n - 1))
            def _():
                cot_copy(b, q, True).wait_send()

            @pl.when((q >= me) & (me > 0))
            def _():
                cot_copy(b, q, False).wait_send()

        return carry

    lax.fori_loop(0, nb, drain, 0)


def line_products(hidden_tan, weights, gate, weight):
    rows, hidden = hidden_tan.shape
    width = weight.shape[1]
    nb = width // (LINE * COLS)
    resident, streams = 3, 2
    bf16, f32 = jnp.bfloat16, jnp.float32
    vmem = pl.BlockSpec(memory_space=pltpu.VMEM)
    sems = pltpu.SemaphoreType.DMA
    return pl.pallas_call(
        functools.partial(line_kernel, nb, resident, streams),
        out_shape=(
            jax.ShapeDtypeStruct((rows, width // LINE), bf16),
            jax.ShapeDtypeStruct((rows, hidden), bf16),
        ),
        in_specs=[vmem, vmem, vmem, pl.BlockSpec(memory_space=pl.ANY)],
        out_specs=(vmem, vmem),
        scratch_shapes=[
            pltpu.VMEM((resident + streams, hidden, LINE * COLS), bf16),
            pltpu.VMEM((nb, LINE, rows, COLS), f32),
            pltpu.VMEM((nb, LINE, rows, COLS), bf16),
            pltpu.VMEM((nb, LINE, rows, COLS), bf16),
            pltpu.VMEM((nb, LINE, rows, COLS), bf16),
            pltpu.VMEM((nb, rows, LINE * COLS), bf16),
            pltpu.VMEM((rows, hidden), f32),
            sems((resident + streams, LINE)),
        ] + [sems((nb, LINE))] * 6,
        compiler_params=pltpu.CompilerParams(
            collective_id=0, has_side_effects=True, vmem_limit_bytes=60 * 1024 * 1024
        ),
        cost_estimate=pl.CostEstimate(
            flops=4 * rows * hidden * width, bytes_accessed=3 * hidden * width, transcendentals=0
        ),
    )(hidden_tan, weights, gate, weight)


def shards(
    feats,
    gate_preactivation,
    row_loss_curvature,
    row_adapter_index,
    row_adapter_position,
    down_projection_weight,
    adapter_input_factors,
    adapter_output_factors,
    iterate_input_factors,
    iterate_output_factors,
    input_factor_gradient,
    output_factor_gradient,
):
    highest_precision = lax.Precision.HIGHEST
    tenant_count = lax.axis_size("tenant")
    local_tenant_count = adapter_input_factors.shape[0]
    row_count = feats.shape[0]
    rows_each = row_count // local_tenant_count
    per_dest = row_count // tenant_count
    d_local = feats.shape[1]
    f_local = gate_preactivation.shape[1]
    target = row_adapter_index // local_tenant_count
    matches = (target[:, None] == jnp.arange(tenant_count, dtype=jnp.int32)[None, :]).astype(
        jnp.int32
    )
    within = jnp.sum((jnp.cumsum(matches, axis=0) - 1) * matches, axis=1)
    send_pos = target * per_dest + within
    send_order = (
        jnp.zeros((row_count,), jnp.int32).at[send_pos].set(jnp.arange(row_count, dtype=jnp.int32))
    )
    place_local = row_adapter_index % local_tenant_count * rows_each + row_adapter_position
    got_x, got_gate, got_weight = (
        lax.all_to_all(feats[send_order], "tenant", split_axis=0, concat_axis=0, tiled=True),
        lax.all_to_all(
            gate_preactivation[send_order], "tenant", split_axis=0, concat_axis=0, tiled=True
        ),
        lax.all_to_all(
            row_loss_curvature[send_order], "tenant", split_axis=0, concat_axis=0, tiled=True
        ),
    )
    arrival = lax.all_to_all(
        place_local[send_order], "tenant", split_axis=0, concat_axis=0, tiled=True
    )
    grouped_input_rows = jnp.zeros_like(got_x).at[arrival].set(got_x)
    grouped_gate = jnp.zeros_like(got_gate).at[arrival].set(got_gate)
    weights = jnp.zeros_like(got_weight).at[arrival].set(got_weight).astype(jnp.float32)
    input_three_axes = grouped_input_rows.reshape(local_tenant_count, rows_each, d_local)
    x_float = input_three_axes.astype(jnp.float32)
    partial_product = jnp.einsum(
        "ake,aex->akx", input_three_axes, adapter_input_factors, preferred_element_type=jnp.float32
    )
    part_q = jnp.einsum("ake,aex->akx", x_float, iterate_input_factors, precision=highest_precision)
    summed_p, summed_q = lax.psum((partial_product, part_q), "tensor")
    project_rows = summed_p / math.sqrt(MODEL_WIDTH)
    lowrank_tangent = summed_q / math.sqrt(MODEL_WIDTH)
    up_tangent = (
        jnp.einsum(
            "wqh,whx->wqx",
            lowrank_tangent,
            adapter_output_factors.astype(jnp.float32),
            precision=highest_precision,
        )
        + jnp.einsum(
            "wqh,whx->wqx", project_rows, iterate_output_factors, precision=highest_precision
        )
    ) / math.sqrt(ADAPTER_RANK)
    gate_act = jax.nn.silu(grouped_gate.astype(jnp.float32)).reshape(
        local_tenant_count, rows_each, f_local
    )
    hidden_tan = (gate_act * up_tangent).astype(jnp.bfloat16).reshape(row_count, f_local)
    if (
        lax.axis_size("tensor") == LINE
        and row_count % 16 == 0
        and f_local % 16 == 0
        and down_projection_weight.shape[1] % (LINE * COLS) == 0
    ):
        row_cot, up_cotangent = line_products(
            hidden_tan, weights[:, None], grouped_gate, down_projection_weight
        )
        up_cotangent = up_cotangent.reshape(local_tenant_count, rows_each, f_local)
    else:
        out_tan = jnp.dot(hidden_tan, down_projection_weight, preferred_element_type=jnp.float32)
        out_share = lax.psum_scatter(out_tan, "tensor", scatter_dimension=1, tiled=True)
        row_cot = (weights[:, None] * out_share).astype(jnp.bfloat16)
        hidden_bar = lax.dot_general(
            lax.all_gather(row_cot, "tensor", axis=1, tiled=True),
            down_projection_weight,
            (((1,), (1,)), ((), ())),
            preferred_element_type=jnp.float32,
        )
        up_cotangent = (gate_act * hidden_bar.reshape(local_tenant_count, rows_each, f_local)).astype(
            jnp.bfloat16
        )
    partial_backward = jnp.einsum(
        "acv,apv->acp", up_cotangent, adapter_output_factors, preferred_element_type=jnp.float32
    )
    lowrank_backward = lax.psum(partial_backward, "tensor") / math.sqrt(ADAPTER_RANK)
    curve_a = jnp.einsum(
        "tsd,tsr->tdr", x_float, lowrank_backward, precision=highest_precision
    ) / math.sqrt(MODEL_WIDTH)
    curvature_output_factor = jnp.einsum(
        "bji,bjw->biw", project_rows, up_cotangent.astype(jnp.float32), precision=highest_precision
    ) / math.sqrt(ADAPTER_RANK)
    new_a = input_factor_gradient + (1.0 - damping) * iterate_input_factors - curve_a / lissa_scale
    new_b = (
        output_factor_gradient
        + (1.0 - damping) * iterate_output_factors
        - curvature_output_factor / lissa_scale
    )
    return (new_a, new_b, row_cot)


def solution(mesh):
    placed = (
        P(("groups", "tenant"), "tensor"),
        P(("groups", "tenant"), "tensor"),
        P(("groups", "tenant")),
        P(("groups", "tenant")),
        P(("groups", "tenant")),
        P("tensor", None),
        P(("groups", "tenant"), "tensor", None),
        P(("groups", "tenant"), None, "tensor"),
        P(("groups", "tenant"), "tensor", None),
        P(("groups", "tenant"), None, "tensor"),
        P(("groups", "tenant"), "tensor", None),
        P(("groups", "tenant"), None, "tensor"),
    )
    return jax.shard_map(
        shards,
        mesh=mesh,
        in_specs=placed,
        out_specs=(
            P(("groups", "tenant"), "tensor", None),
            P(("groups", "tenant"), None, "tensor"),
            P(("groups", "tenant"), "tensor"),
        ),
        check_vma=False,
    )
```

```python
import functools
import math

import jax
import jax.numpy as jnp
from jax import lax
from jax.experimental import pallas as pl
from jax.experimental.pallas import tpu as pltpu
from jax.sharding import PartitionSpec as P

MODEL_WIDTH = 8192
ADAPTER_RANK = 32


damping = 0.05
lissa_scale = 2.0


LINE = 4
COLS = 256
MESH = pl.DeviceIdType.MESH


def line_kernel(
    nb, resident, streams,
    h_ref, w_ref, gate_ref, weight_ref, cot_ref, e_ref,
    wbuf, y, from_left, from_right, outgoing, cot, acc,
    wsem, left_sem, right_sem, sum_send, cot_sem, cot_send_right, cot_send_left,
):
    n = LINE
    me = lax.axis_index("tensor")
    share = nb * COLS
    hidden = h_ref.shape[1]
    streamed = nb - resident

    def fetch(slot, b, q):
        cols = pl.ds(pl.multiple_of(q * share + b * COLS, COLS), COLS)
        return pltpu.make_async_copy(
            weight_ref.at[:, cols], wbuf.at[slot, :, pl.ds(q * COLS, COLS)], wsem.at[slot, q]
        )

    def sum_copy(b, q, to_right):
        return pltpu.make_async_remote_copy(
            src_ref=outgoing.at[b, q],
            dst_ref=(from_left if to_right else from_right).at[b, q],
            send_sem=sum_send.at[b, q],
            recv_sem=(left_sem if to_right else right_sem).at[b, q],
            device_id={"tensor": me + 1 if to_right else me - 1},
            device_id_type=MESH,
        )

    def cot_copy(b, o, to_right):
        block = cot.at[b, :, pl.ds(o * COLS, COLS)]
        return pltpu.make_async_remote_copy(
            src_ref=block,
            dst_ref=block,
            send_sem=(cot_send_right if to_right else cot_send_left).at[b, o],
            recv_sem=cot_sem.at[b, o],
            device_id={"tensor": me + 1 if to_right else me - 1},
            device_id_type=MESH,
        )

    for b in range(resident):
        for q in range(n):
            fetch(b, b, q).start()
    for u in range(streams):
        for q in range(n):
            fetch(resident + u, resident + u, q).start()

    barrier = pltpu.get_barrier_semaphore()
    for neighbour in (lax.rem(me + 1, n), lax.rem(me + n - 1, n)):
        pl.semaphore_signal(barrier, inc=1, device_id={"tensor": neighbour}, device_id_type=MESH)
    pl.semaphore_wait(barrier, 2)

    acc[...] = jnp.zeros_like(acc)

    def advance_sums(i):
        for q in range(n):
            hops = jnp.where(
                me < q, me, jnp.where(me > q, n - 1 - me, jnp.maximum(me, n - 1 - me))
            )
            b = i - 1 - hops

            @pl.when((b >= 0) & (b < nb))
            def _():
                @pl.when((me <= q) & (me > 0))
                def _():
                    sum_copy(b, q, True).wait_recv()
                    y[b, q] += from_left[b, q].astype(jnp.float32)

                @pl.when((me >= q) & (me < n - 1))
                def _():
                    sum_copy(b, q, False).wait_recv()
                    y[b, q] += from_right[b, q].astype(jnp.float32)

                @pl.when(me < q)
                def _():
                    outgoing[b, q] = y[b, q].astype(jnp.bfloat16)
                    sum_copy(b, q, True).start()

                @pl.when(me > q)
                def _():
                    outgoing[b, q] = y[b, q].astype(jnp.bfloat16)
                    sum_copy(b, q, False).start()

                @pl.when(me == q)
                def _():
                    block = (w_ref[...] * y[b, q]).astype(jnp.bfloat16)
                    cot[b, :, q * COLS : (q + 1) * COLS] = block
                    cot_ref[:, pl.ds(pl.multiple_of(b * COLS, COLS), COLS)] = block

                    @pl.when(me < n - 1)
                    def _():
                        cot_copy(b, q, True).start()

                    @pl.when(me > 0)
                    def _():
                        cot_copy(b, q, False).start()

    def advance_cots(i):
        for o in range(n):
            b = i - 1 - max(o, n - 1 - o) - jnp.abs(me - o)

            @pl.when((b >= 0) & (b < nb) & (me != o))
            def _():
                cot_copy(b, o, True).wait_recv()

                @pl.when((me > o) & (me < n - 1))
                def _():
                    cot_copy(b, o, True).start()

                @pl.when((me < o) & (me > 0))
                def _():
                    cot_copy(b, o, False).start()

    def refill(u):
        later = u + streams

        @pl.when((u >= 0) & (later < 2 * streamed))
        def _():
            for q in range(n):
                fetch(resident + later % streams, resident + later % streamed, q).start()

    last_lag = 2 * n - 1

    def step(i, carry):
        advance_sums(i)
        advance_cots(i)

        @pl.when(i < nb)
        def _():
            u = i - resident
            slot = jnp.where(u < 0, i, resident + jnp.maximum(u, 0) % streams)
            for q in range(n):
                fetch(slot, i, q).wait()
                y[i, q] = jnp.dot(
                    h_ref[...],
                    wbuf[slot, :, q * COLS : (q + 1) * COLS],
                    preferred_element_type=jnp.float32,
                )
            refill(u)

        @pl.when(i >= last_lag)
        def _():
            b = i - last_lag
            u = b - resident
            slot = jnp.where(u < 0, b, resident + (jnp.maximum(u, 0) + streamed) % streams)

            @pl.when(u >= 0)
            def _():
                for q in range(n):
                    fetch(slot, b, q).wait()

            for start in range(0, hidden, 512):
                size = min(512, hidden - start)
                acc[:, start : start + size] += lax.dot_general(
                    cot[b],
                    wbuf[slot, start : start + size, :],
                    (((1,), (1,)), ((), ())),
                    preferred_element_type=jnp.float32,
                )

            @pl.when(u >= 0)
            def _():
                refill(u + streamed)

        return carry

    lax.fori_loop(0, nb + last_lag, step, 0)

    for start in range(0, hidden, 512):
        size = min(512, hidden - start)
        gate = gate_ref[:, start : start + size].astype(jnp.float32)
        e_ref[:, start : start + size] = (
            gate / (1.0 + jnp.exp(-gate)) * acc[:, start : start + size]
        ).astype(jnp.bfloat16)

    def drain(b, carry):
        for q in range(n):
            @pl.when(me != q)
            def _():
                sum_copy(b, q, True).wait_send()

            @pl.when((q <= me) & (me < n - 1))
            def _():
                cot_copy(b, q, True).wait_send()

            @pl.when((q >= me) & (me > 0))
            def _():
                cot_copy(b, q, False).wait_send()

        return carry

    lax.fori_loop(0, nb, drain, 0)


def line_products(hidden_tan, weights, gate, weight):
    rows, hidden = hidden_tan.shape
    width = weight.shape[1]
    nb = width // (LINE * COLS)
    resident, streams = 3, 2
    bf16, f32 = jnp.bfloat16, jnp.float32
    vmem = pl.BlockSpec(memory_space=pltpu.VMEM)
    sems = pltpu.SemaphoreType.DMA
    return pl.pallas_call(
        functools.partial(line_kernel, nb, resident, streams),
        out_shape=(
            jax.ShapeDtypeStruct((rows, width // LINE), bf16),
            jax.ShapeDtypeStruct((rows, hidden), bf16),
        ),
        in_specs=[vmem, vmem, vmem, pl.BlockSpec(memory_space=pl.ANY)],
        out_specs=(vmem, vmem),
        scratch_shapes=[
            pltpu.VMEM((resident + streams, hidden, LINE * COLS), bf16),
            pltpu.VMEM((nb, LINE, rows, COLS), f32),
            pltpu.VMEM((nb, LINE, rows, COLS), bf16),
            pltpu.VMEM((nb, LINE, rows, COLS), bf16),
            pltpu.VMEM((nb, LINE, rows, COLS), bf16),
            pltpu.VMEM((nb, rows, LINE * COLS), bf16),
            pltpu.VMEM((rows, hidden), f32),
            sems((resident + streams, LINE)),
        ] + [sems((nb, LINE))] * 6,
        compiler_params=pltpu.CompilerParams(
            collective_id=0, has_side_effects=True, vmem_limit_bytes=60 * 1024 * 1024
        ),
        cost_estimate=pl.CostEstimate(
            flops=4 * rows * hidden * width, bytes_accessed=3 * hidden * width, transcendentals=0
        ),
    )(hidden_tan, weights, gate, weight)


def greet(axis, n):
    me = lax.axis_index(axis)
    barrier = pltpu.get_barrier_semaphore()
    for k in range(1, n):
        pl.semaphore_signal(
            barrier, inc=1, device_id={axis: lax.rem(me + k, n)}, device_id_type=MESH
        )
    pl.semaphore_wait(barrier, n - 1)
    return me


def sum_kernel(x_ref, out_ref, got, send_sem, recv_sem):
    me = greet("tensor", LINE)
    copies = [
        pltpu.make_async_remote_copy(
            src_ref=x_ref,
            dst_ref=got.at[k - 1],
            send_sem=send_sem.at[k - 1],
            recv_sem=recv_sem.at[k - 1],
            device_id={"tensor": lax.rem(me + k, LINE)},
            device_id_type=MESH,
        )
        for k in range(1, LINE)
    ]
    for copy in copies:
        copy.start()
    for copy in copies:
        copy.wait_recv()
    out_ref[...] = x_ref[...] + got[0] + got[1] + got[2]
    for copy in copies:
        copy.wait_send()


def tensor_sum(x, collective_id):
    vmem = pl.BlockSpec(memory_space=pltpu.VMEM)
    return pl.pallas_call(
        sum_kernel,
        out_shape=jax.ShapeDtypeStruct(x.shape, x.dtype),
        in_specs=[vmem],
        out_specs=vmem,
        scratch_shapes=[
            pltpu.VMEM((LINE - 1,) + x.shape, x.dtype),
            pltpu.SemaphoreType.DMA((LINE - 1,)),
            pltpu.SemaphoreType.DMA((LINE - 1,)),
        ],
        compiler_params=pltpu.CompilerParams(
            collective_id=collective_id,
            has_side_effects=True,
            vmem_limit_bytes=16 * 1024 * 1024,
        ),
    )(x)


def exchange_kernel(
    n, x_ref, gate_ref, meta_ref, x_out, gate_out, w_out,
    x_send, gate_send, meta_send, x_got, gate_got, meta_got, send_sem, recv_sem,
):
    bf16, f32 = jnp.bfloat16, jnp.float32
    rows = x_ref.shape[0]
    per = rows // n
    me = lax.axis_index("tenant")

    def moved(select, source):
        return lax.dot_general(
            select, source, (((0,), (0,)), ((), ())), preferred_element_type=f32
        )

    lane = lax.broadcasted_iota(jnp.int32, (rows, rows), 1)
    earlier = (lane < lax.broadcasted_iota(jnp.int32, (rows, rows), 0)).astype(f32).astype(bf16)
    lane = lane.astype(f32)
    meta = meta_ref[...]
    target = meta[:, 1:2]
    matches = (target == lane).astype(f32)
    counts = jnp.dot(earlier, matches.astype(bf16), preferred_element_type=f32)
    within = jnp.sum(counts * matches, axis=1, keepdims=True)
    order = (target * per + within == lane).astype(f32).astype(bf16)

    def spread(source_ref, send_ref):
        width = source_ref.shape[1]
        for start in range(0, width, 512):
            size = min(512, width - start)
            block = moved(order, source_ref[:, start : start + size].astype(bf16)).astype(bf16)
            for t in range(n):
                send_ref[t, :, start : start + size] = block[t * per : (t + 1) * per]

    def copies(which, send_ref, got_ref):
        return [
            pltpu.make_async_remote_copy(
                src_ref=send_ref.at[lax.rem(me + k, n)],
                dst_ref=got_ref.at[k],
                send_sem=send_sem.at[which, k],
                recv_sem=recv_sem.at[which, k],
                device_id={"tenant": lax.rem(me + k, n)},
                device_id_type=MESH,
            )
            for k in range(1, n)
        ]

    spread(meta_ref, meta_send)
    spread(x_ref, x_send)
    greet("tenant", n)
    meta_copies = copies(0, meta_send, meta_got)
    x_copies = copies(1, x_send, x_got)
    gate_copies = copies(2, gate_send, gate_got)
    for copy in meta_copies + x_copies:
        copy.start()
    spread(gate_ref, gate_send)
    for copy in gate_copies:
        copy.start()
    meta_got[0] = meta_send[me]
    x_got[0] = x_send[me]
    gate_got[0] = gate_send[me]

    for copy in meta_copies:
        copy.wait_recv()
    meta_rows = meta_got[...].reshape(rows, meta_ref.shape[1])
    place = (meta_rows[:, 2:3].astype(f32) == lane).astype(f32).astype(bf16)
    w_out[...] = moved(place, meta_rows)[:, 0:1]

    def settle(got_ref, out_ref):
        width = out_ref.shape[1]
        for start in range(0, width, 512):
            size = min(512, width - start)
            block = got_ref[:, :, start : start + size].reshape(rows, size)
            out_ref[:, start : start + size] = moved(place, block).astype(bf16)

    for copy in x_copies:
        copy.wait_recv()
    settle(x_got, x_out)
    for copy in gate_copies:
        copy.wait_recv()
    settle(gate_got, gate_out)
    for copy in meta_copies + x_copies + gate_copies:
        copy.wait_send()


def exchange(n, x, gate, weights, target, place):
    rows = x.shape[0]
    bf16, f32 = jnp.bfloat16, jnp.float32
    column = jnp.arange(128)[None, :]
    meta = jnp.where(
        column == 0,
        weights[:, None].astype(f32),
        jnp.where(
            column == 1,
            target[:, None].astype(f32),
            jnp.where(column == 2, place[:, None].astype(f32), 0.0),
        ),
    )
    vmem = pl.BlockSpec(memory_space=pltpu.VMEM)
    slots = [
        pltpu.VMEM((n, rows // n, width), bf16) for width in (x.shape[1], gate.shape[1], 128)
    ]
    return pl.pallas_call(
        functools.partial(exchange_kernel, n),
        out_shape=(
            jax.ShapeDtypeStruct(x.shape, bf16),
            jax.ShapeDtypeStruct(gate.shape, bf16),
            jax.ShapeDtypeStruct((rows, 1), f32),
        ),
        in_specs=[vmem] * 3,
        out_specs=(vmem,) * 3,
        scratch_shapes=slots + slots + [
            pltpu.SemaphoreType.DMA((3, n)),
            pltpu.SemaphoreType.DMA((3, n)),
        ],
        compiler_params=pltpu.CompilerParams(
            collective_id=3, has_side_effects=True, vmem_limit_bytes=40 * 1024 * 1024
        ),
    )(x, gate, meta)


def shards(
    feats,
    gate_preactivation,
    row_loss_curvature,
    row_adapter_index,
    row_adapter_position,
    down_projection_weight,
    adapter_input_factors,
    adapter_output_factors,
    iterate_input_factors,
    iterate_output_factors,
    input_factor_gradient,
    output_factor_gradient,
):
    highest_precision = lax.Precision.HIGHEST
    tenant_count = lax.axis_size("tenant")
    local_tenant_count = adapter_input_factors.shape[0]
    row_count = feats.shape[0]
    rows_each = row_count // local_tenant_count
    per_dest = row_count // tenant_count
    d_local = feats.shape[1]
    f_local = gate_preactivation.shape[1]
    target = row_adapter_index // local_tenant_count
    place_local = row_adapter_index % local_tenant_count * rows_each + row_adapter_position
    by_kernels = (
        lax.axis_size("tensor") == LINE
        and row_count == 128
        and tenant_count > 1
        and per_dest % 16 == 0
        and f_local % 16 == 0
        and down_projection_weight.shape[1] % (LINE * COLS) == 0
    )
    if by_kernels:
        grouped_input_rows, grouped_gate, weights = exchange(
            tenant_count, feats, gate_preactivation, row_loss_curvature, target, place_local
        )
    else:
        matches = (target[:, None] == jnp.arange(tenant_count, dtype=jnp.int32)[None, :]).astype(
            jnp.int32
        )
        within = jnp.sum((jnp.cumsum(matches, axis=0) - 1) * matches, axis=1)
        send_pos = target * per_dest + within
        send_order = (
            jnp.zeros((row_count,), jnp.int32).at[send_pos].set(jnp.arange(row_count, dtype=jnp.int32))
        )
        got_x, got_gate, got_weight = (
            lax.all_to_all(feats[send_order], "tenant", split_axis=0, concat_axis=0, tiled=True),
            lax.all_to_all(
                gate_preactivation[send_order], "tenant", split_axis=0, concat_axis=0, tiled=True
            ),
            lax.all_to_all(
                row_loss_curvature[send_order], "tenant", split_axis=0, concat_axis=0, tiled=True
            ),
        )
        arrival = lax.all_to_all(
            place_local[send_order], "tenant", split_axis=0, concat_axis=0, tiled=True
        )
        grouped_input_rows = jnp.zeros_like(got_x).at[arrival].set(got_x)
        grouped_gate = jnp.zeros_like(got_gate).at[arrival].set(got_gate)
        weights = jnp.zeros_like(got_weight).at[arrival].set(got_weight).astype(jnp.float32)
        weights = weights[:, None]
    input_three_axes = grouped_input_rows.reshape(local_tenant_count, rows_each, d_local)
    x_float = input_three_axes.astype(jnp.float32)
    partial_product = jnp.einsum(
        "ake,aex->akx", input_three_axes, adapter_input_factors, preferred_element_type=jnp.float32
    )
    part_q = jnp.einsum("ake,aex->akx", x_float, iterate_input_factors, precision=highest_precision)
    if by_kernels:
        both = jnp.concatenate((partial_product, part_q), axis=2)
        both = tensor_sum(both.reshape(row_count, 2 * ADAPTER_RANK), 1)
        both = both.reshape(local_tenant_count, rows_each, 2 * ADAPTER_RANK)
        summed_p, summed_q = both[:, :, :ADAPTER_RANK], both[:, :, ADAPTER_RANK:]
    else:
        summed_p, summed_q = lax.psum((partial_product, part_q), "tensor")
    project_rows = summed_p / math.sqrt(MODEL_WIDTH)
    lowrank_tangent = summed_q / math.sqrt(MODEL_WIDTH)
    up_tangent = (
        jnp.einsum(
            "wqh,whx->wqx",
            lowrank_tangent,
            adapter_output_factors.astype(jnp.float32),
            precision=highest_precision,
        )
        + jnp.einsum(
            "wqh,whx->wqx", project_rows, iterate_output_factors, precision=highest_precision
        )
    ) / math.sqrt(ADAPTER_RANK)
    gate_act = jax.nn.silu(grouped_gate.astype(jnp.float32)).reshape(
        local_tenant_count, rows_each, f_local
    )
    hidden_tan = (gate_act * up_tangent).astype(jnp.bfloat16).reshape(row_count, f_local)
    if by_kernels:
        row_cot, up_cotangent = line_products(
            hidden_tan, weights, grouped_gate, down_projection_weight
        )
        up_cotangent = up_cotangent.reshape(local_tenant_count, rows_each, f_local)
    else:
        out_tan = jnp.dot(hidden_tan, down_projection_weight, preferred_element_type=jnp.float32)
        out_share = lax.psum_scatter(out_tan, "tensor", scatter_dimension=1, tiled=True)
        row_cot = (weights * out_share).astype(jnp.bfloat16)
        hidden_bar = lax.dot_general(
            lax.all_gather(row_cot, "tensor", axis=1, tiled=True),
            down_projection_weight,
            (((1,), (1,)), ((), ())),
            preferred_element_type=jnp.float32,
        )
        up_cotangent = (gate_act * hidden_bar.reshape(local_tenant_count, rows_each, f_local)).astype(
            jnp.bfloat16
        )
    partial_backward = jnp.einsum(
        "acv,apv->acp", up_cotangent, adapter_output_factors, preferred_element_type=jnp.float32
    )
    if by_kernels:
        summed_backward = tensor_sum(
            partial_backward.reshape(row_count, ADAPTER_RANK), 2
        ).reshape(partial_backward.shape)
    else:
        summed_backward = lax.psum(partial_backward, "tensor")
    lowrank_backward = summed_backward / math.sqrt(ADAPTER_RANK)
    curve_a = jnp.einsum(
        "tsd,tsr->tdr", x_float, lowrank_backward, precision=highest_precision
    ) / math.sqrt(MODEL_WIDTH)
    curvature_output_factor = jnp.einsum(
        "bji,bjw->biw", project_rows, up_cotangent.astype(jnp.float32), precision=highest_precision
    ) / math.sqrt(ADAPTER_RANK)
    new_a = input_factor_gradient + (1.0 - damping) * iterate_input_factors - curve_a / lissa_scale
    new_b = (
        output_factor_gradient
        + (1.0 - damping) * iterate_output_factors
        - curvature_output_factor / lissa_scale
    )
    return (new_a, new_b, row_cot)


def solution(mesh):
    placed = (
        P(("groups", "tenant"), "tensor"),
        P(("groups", "tenant"), "tensor"),
        P(("groups", "tenant")),
        P(("groups", "tenant")),
        P(("groups", "tenant")),
        P("tensor", None),
        P(("groups", "tenant"), "tensor", None),
        P(("groups", "tenant"), None, "tensor"),
        P(("groups", "tenant"), "tensor", None),
        P(("groups", "tenant"), None, "tensor"),
        P(("groups", "tenant"), "tensor", None),
        P(("groups", "tenant"), None, "tensor"),
    )
    return jax.shard_map(
        shards,
        mesh=mesh,
        in_specs=placed,
        out_specs=(
            P(("groups", "tenant"), "tensor", None),
            P(("groups", "tenant"), None, "tensor"),
            P(("groups", "tenant"), "tensor"),
        ),
        check_vma=False,
    )
```

```python
import functools
import math

import jax
import jax.numpy as jnp
from jax import lax
from jax.experimental import pallas as pl
from jax.experimental.pallas import tpu as pltpu
from jax.sharding import PartitionSpec as P

MODEL_WIDTH = 8192
ADAPTER_RANK = 32


damping = 0.05
lissa_scale = 2.0


LINE = 4
COLS = 128
MESH = pl.DeviceIdType.MESH


def line_kernel(
    nb, resident, streams,
    h_ref, w_ref, gate_ref, weight_ref, cot_ref, e_ref,
    wbuf, y, from_left, from_right, outgoing, cot, acc,
    wsem, left_sem, right_sem, sum_send, cot_sem, cot_send_right, cot_send_left,
):
    n = LINE
    me = lax.axis_index("tensor")
    share = nb * COLS
    hidden = h_ref.shape[1]
    streamed = nb - resident

    def fetch(slot, b, q):
        cols = pl.ds(pl.multiple_of(q * share + b * COLS, COLS), COLS)
        return pltpu.make_async_copy(
            weight_ref.at[:, cols], wbuf.at[slot, :, pl.ds(q * COLS, COLS)], wsem.at[slot, q]
        )

    def sum_copy(b, q, to_right):
        return pltpu.make_async_remote_copy(
            src_ref=outgoing.at[b, q],
            dst_ref=(from_left if to_right else from_right).at[b, q],
            send_sem=sum_send.at[b, q],
            recv_sem=(left_sem if to_right else right_sem).at[b, q],
            device_id={"tensor": me + 1 if to_right else me - 1},
            device_id_type=MESH,
        )

    def cot_copy(b, o, to_right):
        block = cot.at[b, :, pl.ds(o * COLS, COLS)]
        return pltpu.make_async_remote_copy(
            src_ref=block,
            dst_ref=block,
            send_sem=(cot_send_right if to_right else cot_send_left).at[b, o],
            recv_sem=cot_sem.at[b, o],
            device_id={"tensor": me + 1 if to_right else me - 1},
            device_id_type=MESH,
        )

    for b in range(resident):
        for q in range(n):
            fetch(b, b, q).start()
    for u in range(streams):
        for q in range(n):
            fetch(resident + u, resident + u, q).start()

    barrier = pltpu.get_barrier_semaphore()
    for neighbour in (lax.rem(me + 1, n), lax.rem(me + n - 1, n)):
        pl.semaphore_signal(barrier, inc=1, device_id={"tensor": neighbour}, device_id_type=MESH)
    pl.semaphore_wait(barrier, 2)

    acc[...] = jnp.zeros_like(acc)

    def advance_sums(i):
        for q in range(n):
            hops = jnp.where(
                me < q, me, jnp.where(me > q, n - 1 - me, jnp.maximum(me, n - 1 - me))
            )
            b = i - 1 - hops

            @pl.when((b >= 0) & (b < nb))
            def _():
                @pl.when((me <= q) & (me > 0))
                def _():
                    sum_copy(b, q, True).wait_recv()
                    y[b, q] += from_left[b, q].astype(jnp.float32)

                @pl.when((me >= q) & (me < n - 1))
                def _():
                    sum_copy(b, q, False).wait_recv()
                    y[b, q] += from_right[b, q].astype(jnp.float32)

                @pl.when(me < q)
                def _():
                    outgoing[b, q] = y[b, q].astype(jnp.bfloat16)
                    sum_copy(b, q, True).start()

                @pl.when(me > q)
                def _():
                    outgoing[b, q] = y[b, q].astype(jnp.bfloat16)
                    sum_copy(b, q, False).start()

                @pl.when(me == q)
                def _():
                    block = (w_ref[...] * y[b, q]).astype(jnp.bfloat16)
                    cot[b, :, q * COLS : (q + 1) * COLS] = block
                    cot_ref[:, pl.ds(pl.multiple_of(b * COLS, COLS), COLS)] = block

                    @pl.when(me < n - 1)
                    def _():
                        cot_copy(b, q, True).start()

                    @pl.when(me > 0)
                    def _():
                        cot_copy(b, q, False).start()

    def advance_cots(i):
        for o in range(n):
            b = i - 1 - max(o, n - 1 - o) - jnp.abs(me - o)

            @pl.when((b >= 0) & (b < nb) & (me != o))
            def _():
                cot_copy(b, o, True).wait_recv()

                @pl.when((me > o) & (me < n - 1))
                def _():
                    cot_copy(b, o, True).start()

                @pl.when((me < o) & (me > 0))
                def _():
                    cot_copy(b, o, False).start()

    def refill(u):
        later = u + streams

        @pl.when((u >= 0) & (later < 2 * streamed))
        def _():
            for q in range(n):
                fetch(resident + later % streams, resident + later % streamed, q).start()

    last_lag = 2 * n - 1

    def step(i, carry):
        advance_sums(i)
        advance_cots(i)

        @pl.when(i < nb)
        def _():
            u = i - resident
            slot = jnp.where(u < 0, i, resident + jnp.maximum(u, 0) % streams)
            for q in range(n):
                fetch(slot, i, q).wait()
            product = jnp.dot(h_ref[...], wbuf[slot], preferred_element_type=jnp.float32)
            for q in range(n):
                y[i, q] = product[:, q * COLS : (q + 1) * COLS]
            refill(u)

        @pl.when(i >= last_lag)
        def _():
            b = i - last_lag
            u = b - resident
            slot = jnp.where(u < 0, b, resident + (jnp.maximum(u, 0) + streamed) % streams)

            @pl.when(u >= 0)
            def _():
                for q in range(n):
                    fetch(slot, b, q).wait()

            for start in range(0, hidden, 512):
                size = min(512, hidden - start)
                acc[:, start : start + size] += lax.dot_general(
                    cot[b],
                    wbuf[slot, start : start + size, :],
                    (((1,), (1,)), ((), ())),
                    preferred_element_type=jnp.float32,
                )

            @pl.when(u >= 0)
            def _():
                refill(u + streamed)

        return carry

    lax.fori_loop(0, nb + last_lag, step, 0)

    for start in range(0, hidden, 512):
        size = min(512, hidden - start)
        gate = gate_ref[:, start : start + size].astype(jnp.float32)
        e_ref[:, start : start + size] = (
            gate / (1.0 + jnp.exp(-gate)) * acc[:, start : start + size]
        ).astype(jnp.bfloat16)

    def drain(b, carry):
        for q in range(n):
            @pl.when(me != q)
            def _():
                sum_copy(b, q, True).wait_send()

            @pl.when((q <= me) & (me < n - 1))
            def _():
                cot_copy(b, q, True).wait_send()

            @pl.when((q >= me) & (me > 0))
            def _():
                cot_copy(b, q, False).wait_send()

        return carry

    lax.fori_loop(0, nb, drain, 0)


def line_products(hidden_tan, weights, gate, weight):
    rows, hidden = hidden_tan.shape
    width = weight.shape[1]
    nb = width // (LINE * COLS)
    resident, streams = 6, 4
    bf16, f32 = jnp.bfloat16, jnp.float32
    vmem = pl.BlockSpec(memory_space=pltpu.VMEM)
    sems = pltpu.SemaphoreType.DMA
    return pl.pallas_call(
        functools.partial(line_kernel, nb, resident, streams),
        out_shape=(
            jax.ShapeDtypeStruct((rows, width // LINE), bf16),
            jax.ShapeDtypeStruct((rows, hidden), bf16),
        ),
        in_specs=[vmem, vmem, vmem, pl.BlockSpec(memory_space=pl.ANY)],
        out_specs=(vmem, vmem),
        scratch_shapes=[
            pltpu.VMEM((resident + streams, hidden, LINE * COLS), bf16),
            pltpu.VMEM((nb, LINE, rows, COLS), f32),
            pltpu.VMEM((nb, LINE, rows, COLS), bf16),
            pltpu.VMEM((nb, LINE, rows, COLS), bf16),
            pltpu.VMEM((nb, LINE, rows, COLS), bf16),
            pltpu.VMEM((nb, rows, LINE * COLS), bf16),
            pltpu.VMEM((rows, hidden), f32),
            sems((resident + streams, LINE)),
        ] + [sems((nb, LINE))] * 6,
        compiler_params=pltpu.CompilerParams(
            collective_id=0, has_side_effects=True, vmem_limit_bytes=60 * 1024 * 1024
        ),
        cost_estimate=pl.CostEstimate(
            flops=4 * rows * hidden * width, bytes_accessed=3 * hidden * width, transcendentals=0
        ),
    )(hidden_tan, weights, gate, weight)


def greet(axis, n):
    me = lax.axis_index(axis)
    barrier = pltpu.get_barrier_semaphore()
    for k in range(1, n):
        pl.semaphore_signal(
            barrier, inc=1, device_id={axis: lax.rem(me + k, n)}, device_id_type=MESH
        )
    pl.semaphore_wait(barrier, n - 1)
    return me


def sum_kernel(x_ref, out_ref, got, send_sem, recv_sem):
    me = greet("tensor", LINE)
    copies = [
        pltpu.make_async_remote_copy(
            src_ref=x_ref,
            dst_ref=got.at[k - 1],
            send_sem=send_sem.at[k - 1],
            recv_sem=recv_sem.at[k - 1],
            device_id={"tensor": lax.rem(me + k, LINE)},
            device_id_type=MESH,
        )
        for k in range(1, LINE)
    ]
    for copy in copies:
        copy.start()
    for copy in copies:
        copy.wait_recv()
    out_ref[...] = x_ref[...] + got[0] + got[1] + got[2]
    for copy in copies:
        copy.wait_send()


def tensor_sum(x, collective_id):
    vmem = pl.BlockSpec(memory_space=pltpu.VMEM)
    return pl.pallas_call(
        sum_kernel,
        out_shape=jax.ShapeDtypeStruct(x.shape, x.dtype),
        in_specs=[vmem],
        out_specs=vmem,
        scratch_shapes=[
            pltpu.VMEM((LINE - 1,) + x.shape, x.dtype),
            pltpu.SemaphoreType.DMA((LINE - 1,)),
            pltpu.SemaphoreType.DMA((LINE - 1,)),
        ],
        compiler_params=pltpu.CompilerParams(
            collective_id=collective_id,
            has_side_effects=True,
            vmem_limit_bytes=16 * 1024 * 1024,
        ),
    )(x)


def exchange_kernel(
    n, x_ref, gate_ref, meta_ref, x_out, gate_out, w_out,
    x_send, gate_send, meta_send, x_got, gate_got, meta_got, send_sem, recv_sem,
):
    bf16, f32 = jnp.bfloat16, jnp.float32
    rows = x_ref.shape[0]
    per = rows // n
    me = lax.axis_index("tenant")

    def moved(select, source):
        return lax.dot_general(
            select, source, (((0,), (0,)), ((), ())), preferred_element_type=f32
        )

    lane = lax.broadcasted_iota(jnp.int32, (rows, rows), 1)
    earlier = (lane < lax.broadcasted_iota(jnp.int32, (rows, rows), 0)).astype(f32).astype(bf16)
    lane = lane.astype(f32)
    meta = meta_ref[...]
    target = meta[:, 1:2]
    matches = (target == lane).astype(f32)
    counts = jnp.dot(earlier, matches.astype(bf16), preferred_element_type=f32)
    within = jnp.sum(counts * matches, axis=1, keepdims=True)
    order = (target * per + within == lane).astype(f32).astype(bf16)

    def spread(source_ref, send_ref):
        width = source_ref.shape[1]
        for start in range(0, width, 512):
            size = min(512, width - start)
            block = moved(order, source_ref[:, start : start + size].astype(bf16)).astype(bf16)
            for t in range(n):
                send_ref[t, :, start : start + size] = block[t * per : (t + 1) * per]

    def copies(which, send_ref, got_ref):
        return [
            pltpu.make_async_remote_copy(
                src_ref=send_ref.at[lax.rem(me + k, n)],
                dst_ref=got_ref.at[k],
                send_sem=send_sem.at[which, k],
                recv_sem=recv_sem.at[which, k],
                device_id={"tenant": lax.rem(me + k, n)},
                device_id_type=MESH,
            )
            for k in range(1, n)
        ]

    spread(meta_ref, meta_send)
    spread(x_ref, x_send)
    greet("tenant", n)
    meta_copies = copies(0, meta_send, meta_got)
    x_copies = copies(1, x_send, x_got)
    gate_copies = copies(2, gate_send, gate_got)
    for copy in meta_copies + x_copies:
        copy.start()
    spread(gate_ref, gate_send)
    for copy in gate_copies:
        copy.start()
    meta_got[0] = meta_send[me]
    x_got[0] = x_send[me]
    gate_got[0] = gate_send[me]

    for copy in meta_copies:
        copy.wait_recv()
    meta_rows = meta_got[...].reshape(rows, meta_ref.shape[1])
    place = (meta_rows[:, 2:3].astype(f32) == lane).astype(f32).astype(bf16)
    w_out[...] = moved(place, meta_rows)[:, 0:1]

    def settle(got_ref, out_ref):
        width = out_ref.shape[1]
        for start in range(0, width, 512):
            size = min(512, width - start)
            block = got_ref[:, :, start : start + size].reshape(rows, size)
            out_ref[:, start : start + size] = moved(place, block).astype(bf16)

    for copy in x_copies:
        copy.wait_recv()
    settle(x_got, x_out)
    for copy in gate_copies:
        copy.wait_recv()
    settle(gate_got, gate_out)
    for copy in meta_copies + x_copies + gate_copies:
        copy.wait_send()


def exchange(n, x, gate, weights, target, place):
    rows = x.shape[0]
    bf16, f32 = jnp.bfloat16, jnp.float32
    column = jnp.arange(128)[None, :]
    meta = jnp.where(
        column == 0,
        weights[:, None].astype(f32),
        jnp.where(
            column == 1,
            target[:, None].astype(f32),
            jnp.where(column == 2, place[:, None].astype(f32), 0.0),
        ),
    )
    vmem = pl.BlockSpec(memory_space=pltpu.VMEM)
    slots = [
        pltpu.VMEM((n, rows // n, width), bf16) for width in (x.shape[1], gate.shape[1], 128)
    ]
    return pl.pallas_call(
        functools.partial(exchange_kernel, n),
        out_shape=(
            jax.ShapeDtypeStruct(x.shape, bf16),
            jax.ShapeDtypeStruct(gate.shape, bf16),
            jax.ShapeDtypeStruct((rows, 1), f32),
        ),
        in_specs=[vmem] * 3,
        out_specs=(vmem,) * 3,
        scratch_shapes=slots + slots + [
            pltpu.SemaphoreType.DMA((3, n)),
            pltpu.SemaphoreType.DMA((3, n)),
        ],
        compiler_params=pltpu.CompilerParams(
            collective_id=3, has_side_effects=True, vmem_limit_bytes=40 * 1024 * 1024
        ),
    )(x, gate, meta)


def shards(
    feats,
    gate_preactivation,
    row_loss_curvature,
    row_adapter_index,
    row_adapter_position,
    down_projection_weight,
    adapter_input_factors,
    adapter_output_factors,
    iterate_input_factors,
    iterate_output_factors,
    input_factor_gradient,
    output_factor_gradient,
):
    highest_precision = lax.Precision.HIGHEST
    tenant_count = lax.axis_size("tenant")
    local_tenant_count = adapter_input_factors.shape[0]
    row_count = feats.shape[0]
    rows_each = row_count // local_tenant_count
    per_dest = row_count // tenant_count
    d_local = feats.shape[1]
    f_local = gate_preactivation.shape[1]
    target = row_adapter_index // local_tenant_count
    place_local = row_adapter_index % local_tenant_count * rows_each + row_adapter_position
    by_kernels = (
        lax.axis_size("tensor") == LINE
        and row_count == 128
        and tenant_count > 1
        and per_dest % 16 == 0
        and f_local % 16 == 0
        and down_projection_weight.shape[1] % (LINE * COLS) == 0
        and down_projection_weight.shape[1] >= 12 * LINE * COLS
    )
    if by_kernels:
        grouped_input_rows, grouped_gate, weights = exchange(
            tenant_count, feats, gate_preactivation, row_loss_curvature, target, place_local
        )
    else:
        matches = (target[:, None] == jnp.arange(tenant_count, dtype=jnp.int32)[None, :]).astype(
            jnp.int32
        )
        within = jnp.sum((jnp.cumsum(matches, axis=0) - 1) * matches, axis=1)
        send_pos = target * per_dest + within
        send_order = (
            jnp.zeros((row_count,), jnp.int32).at[send_pos].set(jnp.arange(row_count, dtype=jnp.int32))
        )
        got_x, got_gate, got_weight = (
            lax.all_to_all(feats[send_order], "tenant", split_axis=0, concat_axis=0, tiled=True),
            lax.all_to_all(
                gate_preactivation[send_order], "tenant", split_axis=0, concat_axis=0, tiled=True
            ),
            lax.all_to_all(
                row_loss_curvature[send_order], "tenant", split_axis=0, concat_axis=0, tiled=True
            ),
        )
        arrival = lax.all_to_all(
            place_local[send_order], "tenant", split_axis=0, concat_axis=0, tiled=True
        )
        grouped_input_rows = jnp.zeros_like(got_x).at[arrival].set(got_x)
        grouped_gate = jnp.zeros_like(got_gate).at[arrival].set(got_gate)
        weights = jnp.zeros_like(got_weight).at[arrival].set(got_weight).astype(jnp.float32)
        weights = weights[:, None]
    input_three_axes = grouped_input_rows.reshape(local_tenant_count, rows_each, d_local)
    x_float = input_three_axes.astype(jnp.float32)
    partial_product = jnp.einsum(
        "ake,aex->akx", input_three_axes, adapter_input_factors, preferred_element_type=jnp.float32
    )
    part_q = jnp.einsum("ake,aex->akx", x_float, iterate_input_factors, precision=highest_precision)
    if by_kernels:
        both = jnp.concatenate((partial_product, part_q), axis=2)
        both = tensor_sum(both.reshape(row_count, 2 * ADAPTER_RANK), 1)
        both = both.reshape(local_tenant_count, rows_each, 2 * ADAPTER_RANK)
        summed_p, summed_q = both[:, :, :ADAPTER_RANK], both[:, :, ADAPTER_RANK:]
    else:
        summed_p, summed_q = lax.psum((partial_product, part_q), "tensor")
    project_rows = summed_p / math.sqrt(MODEL_WIDTH)
    lowrank_tangent = summed_q / math.sqrt(MODEL_WIDTH)
    up_tangent = (
        jnp.einsum(
            "wqh,whx->wqx",
            lowrank_tangent,
            adapter_output_factors.astype(jnp.float32),
            precision=highest_precision,
        )
        + jnp.einsum(
            "wqh,whx->wqx", project_rows, iterate_output_factors, precision=highest_precision
        )
    ) / math.sqrt(ADAPTER_RANK)
    gate_act = jax.nn.silu(grouped_gate.astype(jnp.float32)).reshape(
        local_tenant_count, rows_each, f_local
    )
    hidden_tan = (gate_act * up_tangent).astype(jnp.bfloat16).reshape(row_count, f_local)
    if by_kernels:
        row_cot, up_cotangent = line_products(
            hidden_tan, weights, grouped_gate, down_projection_weight
        )
        up_cotangent = up_cotangent.reshape(local_tenant_count, rows_each, f_local)
    else:
        out_tan = jnp.dot(hidden_tan, down_projection_weight, preferred_element_type=jnp.float32)
        out_share = lax.psum_scatter(out_tan, "tensor", scatter_dimension=1, tiled=True)
        row_cot = (weights * out_share).astype(jnp.bfloat16)
        hidden_bar = lax.dot_general(
            lax.all_gather(row_cot, "tensor", axis=1, tiled=True),
            down_projection_weight,
            (((1,), (1,)), ((), ())),
            preferred_element_type=jnp.float32,
        )
        up_cotangent = (gate_act * hidden_bar.reshape(local_tenant_count, rows_each, f_local)).astype(
            jnp.bfloat16
        )
    partial_backward = jnp.einsum(
        "acv,apv->acp", up_cotangent, adapter_output_factors, preferred_element_type=jnp.float32
    )
    if by_kernels:
        summed_backward = tensor_sum(
            partial_backward.reshape(row_count, ADAPTER_RANK), 2
        ).reshape(partial_backward.shape)
    else:
        summed_backward = lax.psum(partial_backward, "tensor")
    lowrank_backward = summed_backward / math.sqrt(ADAPTER_RANK)
    curve_a = jnp.einsum(
        "tsd,tsr->tdr", x_float, lowrank_backward, precision=highest_precision
    ) / math.sqrt(MODEL_WIDTH)
    curvature_output_factor = jnp.einsum(
        "bji,bjw->biw", project_rows, up_cotangent.astype(jnp.float32), precision=highest_precision
    ) / math.sqrt(ADAPTER_RANK)
    new_a = input_factor_gradient + (1.0 - damping) * iterate_input_factors - curve_a / lissa_scale
    new_b = (
        output_factor_gradient
        + (1.0 - damping) * iterate_output_factors
        - curvature_output_factor / lissa_scale
    )
    return (new_a, new_b, row_cot)


def solution(mesh):
    placed = (
        P(("groups", "tenant"), "tensor"),
        P(("groups", "tenant"), "tensor"),
        P(("groups", "tenant")),
        P(("groups", "tenant")),
        P(("groups", "tenant")),
        P("tensor", None),
        P(("groups", "tenant"), "tensor", None),
        P(("groups", "tenant"), None, "tensor"),
        P(("groups", "tenant"), "tensor", None),
        P(("groups", "tenant"), None, "tensor"),
        P(("groups", "tenant"), "tensor", None),
        P(("groups", "tenant"), None, "tensor"),
    )
    return jax.shard_map(
        shards,
        mesh=mesh,
        in_specs=placed,
        out_specs=(
            P(("groups", "tenant"), "tensor", None),
            P(("groups", "tenant"), None, "tensor"),
            P(("groups", "tenant"), "tensor"),
        ),
        check_vma=False,
    )
```
